256 devices in a mesh: depth: 4 (over x), row: 8 (over z), col: 8 (over y, core).
Axes of the slice: x: 4, y: 4, z: 8, core: 2. Of those that a mesh axis runs over, the one named last changes fastest.
Arguments:
- inputs: bfloat16 [512, 12288], P('col', ('depth', 'row')), may hold values from -6 to 6
- w_in: bfloat16 [12288, 24576], P(('depth', 'row'), 'col'), may hold values from -0.0546875 to 0.0546875
- w_out: bfloat16 [24576, 12288], P('col', ('depth', 'row')), may hold values from -0.0390625 to 0.0390625
- grad_out: bfloat16 [512, 12288], P('col', ('depth', 'row')), may hold values from -1.5 to 1.5
Outputs:
- outputs: bfloat16 [512, 12288], P('col', ('depth', 'row'))
- input_grad: bfloat16 [512, 12288], P('col', ('depth', 'row'))
- grad_w_in: bfloat16 [12288, 24576], P(('depth', 'row'), 'col')
- grad_w_out: bfloat16 [24576, 12288], P('col', ('depth', 'row'))
The draws below stay inside these ranges and needn't reach their ends.
All inputs are finite; a program needn't handle non-finite values.
Results may differ from the reference program's by a relative error of at most 0.019.
Values may be sent and summed in bfloat16 or wider, within the bound.
No kernel may reach another device: no remote copies, remote signals or barrier semaphores. Data moves between devices by JAX's collectives and lax.ppermute only.
A program may use at most 128 MiB of HBM per device.

```python
import jax
import jax.numpy as jnp

D = 12288
FF = 24576
TOKENS = 512


def levels(rng, shape, cuts, smallest, high):
    def one(dim, parts):
        steps = jax.random.uniform(jax.random.fold_in(jax.random.fold_in(rng, 6), dim), (parts,), jnp.float32, smallest / len(cuts), high / len(cuts))
        return jnp.repeat(jnp.exp(steps), shape[dim] // parts).reshape((-1,) + (1,) * (len(shape) - dim - 1))

    factor_of = one(*cuts[0])
    for cut in cuts[1:]:
        factor_of = factor_of * one(*cut)
    return factor_of


def scatter_about(rng, shape, spread, reach, split=(), dtype=jnp.bfloat16):
    loudness = levels(rng, shape, split, -0.22, 0.18) if split else 1.0
    result = jax.random.normal(rng, shape, jnp.float32) * spread * loudness
    return jnp.minimum(jnp.maximum(result, -reach), reach).astype(dtype)


def setup_inputs(seed: int = 0) -> dict:
    arg_keys = jax.random.split(jax.random.key(seed), 5)
    return {
        "inputs": scatter_about(arg_keys[0], (TOKENS, D), 1.0, 6.0, ((0, 8), (1, 32))),
        "w_in": scatter_about(arg_keys[1], (D, FF), D ** -0.5, 0.0546875, ((0, 32), (1, 8))),
        "w_out": scatter_about(arg_keys[2], (FF, D), FF ** -0.5, 0.0390625, ((0, 8), (1, 32))),
        "grad_out": scatter_about(arg_keys[3], (TOKENS, D), 0.25, 1.5, ((0, 8), (1, 32))),
    }


def gelu_pair(pre):
    coeff = 0.7978845608
    inner = coeff * (pre + 0.044715 * pre * pre * pre)
    tval = jnp.tanh(inner)
    value = 0.5 * pre * (1.0 + tval)
    slope = 0.5 * (1.0 + tval) + 0.5 * pre * (1.0 - tval * tval) * coeff * (1.0 + 3.0 * 0.044715 * pre * pre)
    return value, slope


def reference(inputs, w_in, w_out, grad_out):
    pre = jnp.dot(inputs, w_in, preferred_element_type=jnp.float32)
    back = jnp.dot(grad_out, w_out.T, preferred_element_type=jnp.float32)
    value, slope = gelu_pair(pre)
    activated = value.astype(jnp.bfloat16)
    hidden_grad = (back * slope).astype(jnp.bfloat16)
    outputs = jnp.dot(activated, w_out, preferred_element_type=jnp.float32).astype(jnp.bfloat16)
    input_grad = jnp.dot(hidden_grad, w_in.T, preferred_element_type=jnp.float32).astype(jnp.bfloat16)
    grad_w_in = jnp.dot(inputs.T, hidden_grad, preferred_element_type=jnp.float32).astype(jnp.bfloat16)
    grad_w_out = jnp.dot(activated.T, grad_out, preferred_element_type=jnp.float32).astype(jnp.bfloat16)
    return (outputs, input_grad, grad_w_in, grad_w_out)
```

```python
import jax
import jax.numpy as jnp
from jax import lax
from jax.experimental import pallas as pl
from jax.experimental.pallas import tpu as pltpu
from jax.sharding import PartitionSpec as P

BF = jnp.bfloat16
F32 = jnp.float32


def gelu_pair(pre):
    coeff = 0.7978845608
    inner = coeff * (pre + 0.044715 * pre * pre * pre)
    tval = jnp.tanh(inner)
    value = 0.5 * pre * (1.0 + tval)
    slope = 0.5 * (1.0 + tval) + 0.5 * pre * (1.0 - tval * tval) * coeff * (
        1.0 + 3.0 * 0.044715 * pre * pre
    )
    return (value, slope)


def shift(x, axis, k, n):
    return lax.ppermute(x, axis, [(i, (i + k) % n) for i in range(n)])


def shift_y(x, k):
    return lax.ppermute(x, "col", [(i, (i + 2 * k) % 8) for i in range(8)])


def swap_core(x):
    return lax.ppermute(x, "col", [(i, i ^ 1) for i in range(8)])


def ring_reduce(part, axis, n):
    half = n // 2
    far = part(half).astype(BF)
    right = shift(far[0], axis, 1, n)
    left = shift(far[1], axis, -1, n)
    for step in range(1, half):
        dist = half - step
        to_right, to_left = part(dist), part(-dist)
        if step == 1:
            to_right = jnp.stack([to_right[0] + right, to_right[1]])
            to_left = jnp.stack([to_left[0], to_left[1] + left])
        else:
            to_right = to_right + right
            to_left = to_left + left
        right = shift(to_right.astype(BF), axis, 1, n)
        left = shift(to_left.astype(BF), axis, -1, n)
    return part(0) + right.astype(F32) + left.astype(F32)


def ring_gather(own, axis, n, put):
    half = n // 2
    put(0, None, own)
    right = left = own
    for step in range(1, half):
        right = shift(right, axis, 1, n)
        left = shift(left, axis, -1, n)
        put(-step, None, right)
        put(step, None, left)
    right = shift(right[0], axis, 1, n)
    left = shift(left[1], axis, -1, n)
    put(half, 0, right)
    put(half, 1, left)


def partial_kernel(tok_ref, w_in_ref, w_out_ref, out_ref):
    out_ref[0] = jnp.dot(tok_ref[0], w_in_ref[...], preferred_element_type=F32)
    out_ref[1] = lax.dot_general(
        tok_ref[1], w_out_ref[...], (((1,), (1,)), ((), ())), preferred_element_type=F32
    )


def partials(tok, w_in, w_out):
    _, rows, feat = tok.shape
    hid = w_in.shape[1]
    step = 512
    return pl.pallas_call(
        partial_kernel,
        grid=(hid // step,),
        in_specs=[
            pl.BlockSpec((2, rows, feat), lambda i: (0, 0, 0)),
            pl.BlockSpec((feat, step), lambda i: (0, i)),
            pl.BlockSpec((step, feat), lambda i: (i, 0)),
        ],
        out_specs=pl.BlockSpec((2, rows, step), lambda i: (0, 0, i)),
        out_shape=jax.ShapeDtypeStruct((2, rows, hid), F32),
        cost_estimate=pl.CostEstimate(
            flops=4 * rows * feat * hid,
            bytes_accessed=4 * feat * hid + 8 * rows * hid + 4 * rows * feat,
            transcendentals=0,
        ),
        compiler_params=pltpu.CompilerParams(vmem_limit_bytes=32 * 1024 * 1024),
    )(tok, w_in, w_out)


def rows_of(x, start, count):
    return lax.dynamic_slice_in_dim(x, start, count, axis=1)


def shards(inputs, w_in, w_out, grad_out):
    x_at, z_at = lax.axis_index("depth"), lax.axis_index("row")
    own = jnp.stack([inputs, grad_out])
    rows = inputs.shape[0]

    near = [own] + [shift_y(own, -j) for j in (1, 2, 3)]
    mate0 = swap_core(own)
    mates = swap_core(jnp.concatenate(near[1:], axis=1))
    tok_a = jnp.concatenate([own, mate0, near[1], mates[:, :rows]], axis=1)
    tok_b = jnp.concatenate([near[2], mates[:, rows : 2 * rows], near[3], mates[:, 2 * rows :]], axis=1)

    total = 4 * rows
    part_a = partials(tok_a, w_in, w_out)
    part_b = partials(tok_b, w_in, w_out)
    tiny = total // 32

    mid_a = ring_reduce(
        lambda k: rows_of(part_a, ((x_at + k) % 4) * (total // 4), total // 4), "depth", 4
    )
    sum_a = ring_reduce(lambda k: rows_of(mid_a, ((z_at + k) % 8) * tiny, tiny), "row", 8)
    mid_b = ring_reduce(
        lambda k: rows_of(part_b, ((z_at + k) % 8) * (total // 8), total // 8), "row", 8
    )
    sum_b = ring_reduce(lambda k: rows_of(mid_b, ((x_at + k) % 4) * tiny, tiny), "depth", 4)

    def activate(total_sum):
        value, slope = gelu_pair(total_sum[0])
        return jnp.stack([value.astype(BF), (total_sum[1] * slope).astype(BF)])

    act_a, act_b = activate(sum_a), activate(sum_b)

    def gather(own_block, axis, n, at, size):
        box = [jnp.zeros((2, size * n, own_block.shape[2]), BF)]

        def put(k, which, block):
            start = ((at + k) % n) * size
            if which is None:
                box[0] = lax.dynamic_update_slice(box[0], block, (0, start, 0))
            else:
                box[0] = lax.dynamic_update_slice(box[0], block[None], (which, start, 0))

        ring_gather(own_block, axis, n, put)
        return box[0]

    hid_a = gather(gather(act_a, "row", 8, z_at, tiny), "depth", 4, x_at, total // 4)
    hid_b = gather(gather(act_b, "depth", 4, x_at, tiny), "row", 8, z_at, total // 8)

    def back_out(hid):
        out = jnp.dot(hid[0], w_out, preferred_element_type=F32)
        grad = lax.dot_general(hid[1], w_in, (((1,), (1,)), ((), ())), preferred_element_type=F32)
        return jnp.stack([out, grad])

    out_a, out_b = back_out(hid_a), back_out(hid_b)

    def block(x, i):
        return x[:, i * rows : (i + 1) * rows]

    def paired(out):
        other = swap_core(jnp.concatenate([block(out, 1), block(out, 3)], axis=1).astype(BF))
        return block(out, 0) + other[:, :rows], block(out, 2) + other[:, rows:]

    here, plus1 = paired(out_a)
    plus2, plus3 = paired(out_b)
    final = (
        here
        + shift_y(plus1.astype(BF), 1)
        + shift_y(plus2.astype(BF), 2)
        + shift_y(plus3.astype(BF), 3)
    ).astype(BF)

    hid = jnp.concatenate([hid_a, hid_b], axis=1)
    tok = jnp.concatenate([tok_a, tok_b], axis=1)
    grad_w_in = lax.dot_general(
        tok[0], hid[1], (((0,), (0,)), ((), ())), preferred_element_type=F32
    ).astype(BF)
    grad_w_out = lax.dot_general(
        hid[0], tok[1], (((0,), (0,)), ((), ())), preferred_element_type=F32
    ).astype(BF)
    return (final[0], final[1], grad_w_in, grad_w_out)


def solution(mesh):
    return jax.shard_map(
        shards,
        mesh=mesh,
        in_specs=(
            P("col", ("depth", "row")),
            P(("depth", "row"), "col"),
            P("col", ("depth", "row")),
            P("col", ("depth", "row")),
        ),
        out_specs=(
            P("col", ("depth", "row")),
            P("col", ("depth", "row")),
            P(("depth", "row"), "col"),
            P("col", ("depth", "row")),
        ),
        check_vma=False,
    )
```

```python
import functools

import jax
import jax.numpy as jnp
from jax import lax
from jax.experimental import pallas as pl
from jax.experimental.pallas import tpu as pltpu
from jax.sharding import PartitionSpec as P

BF = jnp.bfloat16
F32 = jnp.float32


def gelu_pair(pre):
    coeff = 0.7978845608
    inner = coeff * (pre + 0.044715 * pre * pre * pre)
    tval = jnp.tanh(inner)
    value = 0.5 * pre * (1.0 + tval)
    slope = 0.5 * (1.0 + tval) + 0.5 * pre * (1.0 - tval * tval) * coeff * (
        1.0 + 3.0 * 0.044715 * pre * pre
    )
    return (value, slope)


def sign_of(core):
    return 1 if core % 2 == 0 else -1


def shift(x, axis, k, n):
    return lax.ppermute(x, axis, [(i, (i + k) % n) for i in range(n)])


def spread(x, axis, n, way):
    return lax.ppermute(
        x,
        (axis, "col"),
        [
            (i * 8 + c, ((i + way * sign_of(c)) % n) * 8 + c)
            for i in range(n)
            for c in range(8)
        ],
    )


def mate_of(i, core):
    return (i + (1 if i % 2 == 0 else -1) * sign_of(core)) % 8


def swap_mate(x):
    return lax.ppermute(
        x, ("row", "col"), [(i * 8 + c, mate_of(i, c) * 8 + c) for i in range(8) for c in range(8)]
    )


def shift_y(x, k):
    return lax.ppermute(x, "col", [(i, (i + 2 * k) % 8) for i in range(8)])


def swap_core(x):
    return lax.ppermute(x, "col", [(i, i ^ 1) for i in range(8)])


def add(x, y):
    return (x.astype(F32) + y.astype(F32)).astype(BF)


def ring_reduce(part, axis, n):
    half = n // 2
    near = far = None
    for dist in range(half, 0, -1):
        term = part(dist)
        far = spread(term.astype(BF) if far is None else add(term, far), axis, n, 1)
        if dist > 1:
            term = part(1 - dist)
            near = spread(term.astype(BF) if near is None else add(term, near), axis, n, -1)
    return far, near


def ring_gather(own, axis, n, put):
    half = n // 2
    far = near = own
    for dist in range(1, half + 1):
        far = spread(far, axis, n, 1)
        put(-dist, far)
        if dist < half:
            near = spread(near, axis, n, -1)
            put(dist, near)


MIB = 1024 * 1024


def small(limit=8):
    return pltpu.CompilerParams(vmem_limit_bytes=limit * MIB)


def pack(inputs, grad_out):
    def body(x_ref, g_ref, out_ref):
        out_ref[0] = x_ref[...]
        out_ref[1] = g_ref[...]

    return pl.pallas_call(
        body,
        out_shape=jax.ShapeDtypeStruct((2,) + inputs.shape, BF),
        compiler_params=small(4),
    )(inputs, grad_out)


def gather_rows(blocks):
    _, eighth, feat = blocks[0].shape

    def body(*refs):
        for i, ref in enumerate(refs[:-1]):
            refs[-1][:, i * eighth : (i + 1) * eighth, :] = ref[...]

    return pl.pallas_call(
        body,
        out_shape=jax.ShapeDtypeStruct((2, len(blocks) * eighth, feat), BF),
        compiler_params=small(4),
    )(*blocks)


def partial_kernel(tok_ref, w_in_ref, w_out_ref, out_ref):
    out_ref[0] = jnp.dot(tok_ref[0], w_in_ref[...], preferred_element_type=F32).astype(BF)
    out_ref[1] = lax.dot_general(
        tok_ref[1], w_out_ref[...], (((1,), (1,)), ((), ())), preferred_element_type=F32
    ).astype(BF)


def partials(tok, w_in, w_out):
    _, rows, feat = tok.shape
    hid = w_in.shape[1]
    step = 512
    return pl.pallas_call(
        partial_kernel,
        grid=(hid // step,),
        in_specs=[
            pl.BlockSpec((2, rows, feat), lambda i: (0, 0, 0)),
            pl.BlockSpec((feat, step), lambda i: (0, i)),
            pl.BlockSpec((step, feat), lambda i: (i, 0)),
        ],
        out_specs=pl.BlockSpec((2, rows, step), lambda i: (0, 0, i)),
        out_shape=jax.ShapeDtypeStruct((2, rows, hid), BF),
        cost_estimate=pl.CostEstimate(
            flops=4 * rows * feat * hid,
            bytes_accessed=4 * feat * hid + 4 * rows * hid + 4 * rows * feat,
            transcendentals=0,
        ),
        compiler_params=small(14),
    )(
        tok,
        pltpu.with_memory_space_constraint(w_in, pltpu.HBM),
        pltpu.with_memory_space_constraint(w_out, pltpu.HBM),
    )


def after(x, *others):
    return lax.optimization_barrier((x,) + others)[0]


def halves_reduce(part, axis):
    two, one, back = part(2), part(1), part(-1)
    far0 = spread(two[0], axis, 4, 1)
    near0 = spread(back[0], axis, 4, -1)
    far1 = spread(after(two[1], far0, near0), axis, 4, 1)
    near1 = spread(after(back[1], far0, near0), axis, 4, -1)
    far0 = spread(after(add(one[0], far0), far1, near1), axis, 4, 1)
    far1 = spread(after(add(one[1], far1), far0), axis, 4, 1)
    return far0, far1, near0, near1


def halves_gather(blocks, axis, put):
    far0 = spread(blocks[0], axis, 4, 1)
    near0 = spread(blocks[0], axis, 4, -1)
    far1 = spread(after(blocks[1], far0, near0), axis, 4, 1)
    near1 = spread(after(blocks[1], far0, near0), axis, 4, -1)
    put(-1, 0, far0)
    put(1, 0, near0)
    put(-1, 1, far1)
    put(1, 1, near1)
    last0 = spread(after(far0, far1, near1), axis, 4, 1)
    put(-2, 0, last0)
    put(-2, 1, spread(after(far1, last0), axis, 4, 1))


def split_kernel(which, at_ref, part, far0, far1, near0, near1, out_ref):
    cols = out_ref.shape[3]
    for m in range(4):
        start = pl.multiple_of(lax.rem(at_ref[which] + 2 * m, 8) * cols, 128)
        now = pl.ds(start, cols)
        for i, far, near in ((0, far0, near0), (1, far1, near1)):
            value = part[i, :, now].astype(F32) + far[:, now].astype(F32) + near[:, now].astype(F32)
            out_ref[m, i] = value.astype(out_ref.dtype)


def split_pairs(part, sums, at, which, dtype):
    rows, hid = sums[0].shape
    cols = hid // 8
    whole = pl.BlockSpec((rows, hid), lambda i, at_ref: (0, 0))
    return pl.pallas_call(
        functools.partial(split_kernel, which),
        grid_spec=pltpu.PrefetchScalarGridSpec(
            num_scalar_prefetch=1,
            grid=(1,),
            in_specs=[pl.BlockSpec((2, rows, hid), lambda i, at_ref: (0, at_ref[0], 0))] + [whole] * 4,
            out_specs=pl.BlockSpec((4, 2, rows, cols), lambda i, at_ref: (0, 0, 0, 0)),
        ),
        out_shape=jax.ShapeDtypeStruct((4, 2, rows, cols), dtype),
        compiler_params=small(12),
    )(at, part, *sums)


def join_kernel(array, at_ref, mine, theirs, out_ref):
    cols = mine.shape[3]
    for m in range(4):
        for which, ref in ((1, mine), (2, theirs)):
            start = pl.multiple_of(lax.rem(at_ref[which] + 2 * m, 8) * cols, 128)
            out_ref[:, pl.ds(start, cols)] = ref[m, array]


def join_pairs(mine, theirs, at, array):
    _, _, rows, cols = mine.shape
    return pl.pallas_call(
        functools.partial(join_kernel, array),
        in_specs=[pl.BlockSpec(memory_space=pltpu.SMEM)] + [pl.BlockSpec(memory_space=pltpu.VMEM)] * 2,
        out_shape=jax.ShapeDtypeStruct((rows, 8 * cols), BF),
        compiler_params=small(8),
    )(at, mine, theirs)


def place(block, start, shape, dim):
    def body(at_ref, block_ref, out_ref):
        size = block_ref.shape[dim]
        now = pl.ds(pl.multiple_of(at_ref[0], size), size)
        out_ref[(slice(None),) * dim + (now,)] = block_ref[...]

    return pl.pallas_call(
        body,
        in_specs=[pl.BlockSpec(memory_space=pltpu.SMEM), pl.BlockSpec(memory_space=pltpu.VMEM)],
        out_shape=jax.ShapeDtypeStruct(shape, BF),
        compiler_params=small(6),
    )(jnp.reshape(start, (1,)).astype(jnp.int32), block)


def activate(total_sum):
    value, slope = gelu_pair(total_sum[0])
    return jnp.stack([value.astype(BF), (total_sum[1] * slope).astype(BF)])


def rows_of(x, start, count):
    return lax.dynamic_slice_in_dim(x, start, count, axis=1)


def shards(inputs, w_in, w_out, grad_out):
    x_at, z_at = lax.axis_index("depth"), lax.axis_index("row")
    core = lax.rem(lax.axis_index("col"), 2)
    way = 1 - 2 * core
    mate = lax.rem(z_at + 8 + (1 - 2 * lax.rem(z_at, 2)) * way, 8)
    at = jnp.stack([x_at, z_at, mate]).astype(jnp.int32)
    own = pack(inputs, grad_out)
    rows = inputs.shape[0]
    hid = w_in.shape[1]

    near = [own] + [shift_y(own, -j) for j in (1, 2, 3)]
    both_cores = [b for j in range(4) for b in (near[j], swap_core(near[j]))]

    total = 4 * rows
    rows_a, rows_b = total // 4, total // 8
    tok = gather_rows(both_cores)
    part = partials(tok, w_in, w_out)

    def index_a(k):
        return lax.rem(x_at + 8 + k * way, 4) * rows_a

    def index_b(k):
        return lax.rem(z_at + 16 + k * way, 8) * rows_b

    sums_a = halves_reduce(lambda k: rows_of(part, index_a(k), rows_a), "depth")
    far_b, near_b = ring_reduce(lambda k: rows_of(part, total + index_b(k), rows_b), "row", 8)

    send = split_pairs(part, sums_a, at, 2, BF)
    keep = split_pairs(part, sums_a, at, 1, F32)
    both = keep + swap_mate(send)
    sum_a = both[0]
    for m in (1, 2, 3):
        sum_a = sum_a + shift(both[m].astype(BF), "row", 2 * m, 8)

    cols_b = hid // 4

    def column_b(k):
        return lax.rem(x_at + 8 + k * way, 4) * cols_b

    def part_x(k):
        start = column_b(k)
        rows_now = lax.dynamic_slice(
            part, (0, total + z_at * rows_b, start), (2, rows_b, cols_b)
        )
        return rows_now.astype(F32) + sum(
            lax.dynamic_slice_in_dim(v, start, cols_b, axis=2).astype(F32) for v in (far_b, near_b)
        )

    far_x, near_x = ring_reduce(part_x, "depth", 4)
    sum_b = part_x(0) + far_x + near_x

    act_a, act_b = activate(sum_a), activate(sum_b)

    mine = jnp.stack(
        [act_a] + [shift(act_a, "row", -2 * m, 8) for m in (1, 2, 3)]
    )
    theirs = swap_mate(mine)
    blocks_a = [join_pairs(mine, theirs, at, i) for i in (0, 1)]
    box_a = [place(blocks_a[i], index_a(0), (total, hid), 0) for i in (0, 1)]

    def put_a(k, i, got):
        box_a[i] = lax.dynamic_update_slice(box_a[i], got, (index_a(k), 0))

    halves_gather(blocks_a, "depth", put_a)

    box_b = [place(act_b, column_b(0), (2, rows_b, hid), 2)]

    def put_x(k, got):
        box_b[0] = lax.dynamic_update_slice(box_b[0], got, (0, 0, column_b(k)))

    ring_gather(act_b, "depth", 4, put_x)
    block_b = box_b[0]
    box_b = [place(block_b, index_b(0), (2, total, hid), 1)]

    def put_b(k, got):
        box_b[0] = lax.dynamic_update_slice(box_b[0], got, (0, index_b(k), 0))

    ring_gather(block_b, "row", 8, put_b)
    hid_b = box_b[0]

    def back_out(act, hidden_grad):
        out = jnp.dot(act, w_out, preferred_element_type=F32)
        grad = lax.dot_general(hidden_grad, w_in, (((1,), (1,)), ((), ())), preferred_element_type=F32)
        return jnp.stack([out, grad])

    out_a, out_b = back_out(*box_a), back_out(hid_b[0], hid_b[1])

    def block(x, i):
        return x[:, i * rows : (i + 1) * rows]

    def paired(out):
        other = swap_core(jnp.concatenate([block(out, 1), block(out, 3)], axis=1).astype(BF))
        return block(out, 0) + other[:, :rows], block(out, 2) + other[:, rows:]

    here, plus1 = paired(out_a)
    plus2, plus3 = paired(out_b)
    final = (
        here
        + shift_y(plus1.astype(BF), 1)
        + shift_y(plus2.astype(BF), 2)
        + shift_y(plus3.astype(BF), 3)
    ).astype(BF)

    act, hidden_grad = [jnp.concatenate([box_a[i], hid_b[i]], axis=0) for i in (0, 1)]
    grad_w_in = lax.dot_general(
        tok[0], hidden_grad, (((0,), (0,)), ((), ())), preferred_element_type=F32
    ).astype(BF)
    grad_w_out = lax.dot_general(
        act, tok[1], (((0,), (0,)), ((), ())), preferred_element_type=F32
    ).astype(BF)
    return (final[0], final[1], grad_w_in, grad_w_out)


def solution(mesh):
    return jax.shard_map(
        shards,
        mesh=mesh,
        in_specs=(
            P("col", ("depth", "row")),
            P(("depth", "row"), "col"),
            P("col", ("depth", "row")),
            P("col", ("depth", "row")),
        ),
        out_specs=(
            P("col", ("depth", "row")),
            P("col", ("depth", "row")),
            P(("depth", "row"), "col"),
            P("col", ("depth", "row")),
        ),
        check_vma=False,
    )
```

```python
import functools

import jax
import jax.numpy as jnp
import numpy as np
from jax import lax
from jax.experimental import pallas as pl
from jax.experimental.pallas import tpu as pltpu
from jax.sharding import PartitionSpec as P

BF = jnp.bfloat16
F32 = jnp.float32


def gelu_pair(pre):
    coeff = 0.7978845608
    inner = coeff * (pre + 0.044715 * pre * pre * pre)
    tval = jnp.tanh(inner)
    value = 0.5 * pre * (1.0 + tval)
    slope = 0.5 * (1.0 + tval) + 0.5 * pre * (1.0 - tval * tval) * coeff * (
        1.0 + 3.0 * 0.044715 * pre * pre
    )
    return (value, slope)


def shift_y(x, k):
    return lax.ppermute(x, "col", [(i, (i + 2 * k) % 8) for i in range(8)])


def swap_core(x):
    return lax.ppermute(x, "col", [(i, i ^ 1) for i in range(8)])


def together(pair):
    return lax.optimization_barrier(tuple(pair))


def add(x, y):
    return (x.astype(F32) + y.astype(F32)).astype(BF)


def after(x, *others):
    return lax.optimization_barrier((x,) + others)[0]


PAIRS_X = ([1, 0, 3, 2], [3, 2, 1, 0])
PAIRS_Z = ([1, 0, 3, 2, 5, 4, 7, 6], [7, 2, 1, 4, 3, 6, 5, 0], [3, 6, 5, 0, 7, 2, 1, 4])
STEPS = (
    (("x", 0), ("x", 1), ("z", 0), ("z", 1), ("z", 2)),
    (("z", 0), ("z", 1), ("x", 0), ("x", 1), ("z", 2)),
)


def ring_of(i, array, n):
    return i if array == 0 else (n - i) % n


def partner_of(d, r, core, step, array):
    axis, k = STEPS[core][step]
    if axis == "x":
        return ring_of(PAIRS_X[k][ring_of(d, array, 4)], array, 4), r
    return d, ring_of(PAIRS_Z[k][ring_of(r, array, 8)], array, 8)


def order_of(d, r, core, array, step):
    if step == 5:
        return [d * 8 + r]
    return order_of(*partner_of(d, r, core, step, array), core, array, step + 1) + order_of(
        d, r, core, array, step + 1
    )


def orders():
    return np.array(
        [
            [
                [[order_of(d, r, core, array, 0) for array in (0, 1)] for r in range(8)]
                for d in range(4)
            ]
            for core in (0, 1)
        ],
        np.int32,
    )


def exchange(x, step, array):
    pairs = []
    for d in range(4):
        for r in range(8):
            for c in range(8):
                d2, r2 = partner_of(d, r, c % 2, step, array)
                pairs.append((d * 64 + r * 8 + c, d2 * 64 + r2 * 8 + c))
    return lax.ppermute(x, ("depth", "row", "col"), pairs)


MIB = 1024 * 1024


def small(limit=8):
    return pltpu.CompilerParams(vmem_limit_bytes=limit * MIB)


VMEM = pl.BlockSpec(memory_space=pltpu.VMEM)


def pack(inputs, grad_out):
    feat = inputs.shape[1]

    def body(x_ref, g_ref, out_ref):
        out_ref[:, :feat] = x_ref[...]
        out_ref[:, feat:] = g_ref[...]

    return pl.pallas_call(
        body,
        out_shape=jax.ShapeDtypeStruct((inputs.shape[0], 2 * feat), BF),
        compiler_params=small(4),
    )(inputs, grad_out)


def partials(tok, array, piece, w_here, w_there):
    rows = tok.shape[0] // 2
    hid = w_here.shape[1 - array]
    step = 768

    def body(tok_ref, here_ref, there_ref, out_ref):
        now = tok_ref[piece * rows : (piece + 1) * rows, :]
        for base, ref in ((0, here_ref), (hid, there_ref)):
            for i in range(0, hid, step):
                if array == 0:
                    value = jnp.dot(now, ref[:, i : i + step], preferred_element_type=F32)
                else:
                    value = lax.dot_general(
                        ref[i : i + step, :], now, (((1,), (1,)), ((), ())), preferred_element_type=F32
                    ).T
                out_ref[:, base + i : base + i + step] = value.astype(BF)

    return pl.pallas_call(
        body,
        in_specs=[VMEM] * 3,
        out_specs=VMEM,
        out_shape=jax.ShapeDtypeStruct((rows, 2 * hid), BF),
        cost_estimate=pl.CostEstimate(
            flops=4 * rows * w_here.size, bytes_accessed=4 * rows * hid, transcendentals=0
        ),
        compiler_params=small(16),
    )(tok, w_here, w_there)


def products(act, hidden_grad, w_in, w_in2, w_out, w_out2):
    rows, hid = act.shape[0], w_in.shape[1]
    feat = w_in.shape[0]

    def body(a_ref, h_ref, in_ref, in2_ref, out_w_ref, out2_ref, out_ref):
        out_ref[0] = jnp.dot(a_ref[:, :hid], out_w_ref[...], preferred_element_type=F32) + jnp.dot(
            a_ref[:, hid:], out2_ref[...], preferred_element_type=F32
        )
        turned = (((1,), (1,)), ((), ()))
        out_ref[1] = (
            lax.dot_general(in_ref[...], h_ref[:, :hid], turned, preferred_element_type=F32)
            + lax.dot_general(in2_ref[...], h_ref[:, hid:], turned, preferred_element_type=F32)
        ).T

    return pl.pallas_call(
        body,
        in_specs=[VMEM] * 6,
        out_specs=VMEM,
        out_shape=jax.ShapeDtypeStruct((2, rows, feat), F32),
        cost_estimate=pl.CostEstimate(
            flops=8 * rows * w_in.size, bytes_accessed=8 * rows * hid, transcendentals=0
        ),
        compiler_params=small(24),
    )(act, hidden_grad, w_in, w_in2, w_out, w_out2)


def shards(inputs, w_in, w_out, grad_out):
    x_at, z_at = lax.axis_index("depth"), lax.axis_index("row")
    core = lax.rem(lax.axis_index("col"), 2)
    rows, feat = inputs.shape
    hid = w_in.shape[1]
    both = (0, 1)

    own = pack(inputs, grad_out)
    w_in2, w_out2 = swap_core(w_in), swap_core(w_out)
    tokens = jnp.concatenate([own] + [shift_y(own, -j) for j in (1, 2, 3)], axis=0)
    order = jnp.asarray(orders())[core, x_at, z_at]
    size = 4 * rows // 32
    wanted = (order[:, :, None] * size + jnp.arange(size, dtype=jnp.int32)).reshape(2, 4 * rows)
    pick = (wanted[:, :, None] == jnp.arange(4 * rows, dtype=jnp.int32)).astype(BF)
    ordered = [jnp.dot(pick[a], tokens, preferred_element_type=F32).astype(BF) for a in both]
    tok = (ordered[0][:, :feat], ordered[1][:, feat:])
    weights = ((w_in, w_in2), (w_out, w_out2))
    send = [partials(tok[a], a, 0, *weights[a]) for a in both]
    keep = [partials(tok[a], a, 1, *weights[a]) for a in both]

    for step in range(5):
        got = [exchange(send[a], step, a) for a in both]
        if step < 2:
            got = together(got)
        left = keep[0].shape[0] // 2
        if step == 4:
            total = [keep[a].astype(F32) + got[a] for a in both]
        else:
            send = [add(keep[a][:left], got[a][:left]) for a in both]
            keep = [keep[a][left:].astype(F32) + got[a][left:] for a in both]

    value, slope = gelu_pair(total[0])
    held = [value.astype(BF), (total[1] * slope).astype(BF)]

    for step in (4, 3, 2, 1, 0):
        got = [exchange(held[a], step, a) for a in both]
        if step < 2:
            got = together(got)
        if step == 0:
            two, rest = held, got
        else:
            held = [jnp.concatenate([got[a], held[a]], axis=0) for a in both]

    all_weights = (w_in, w_in2, w_out, w_out2)
    late, early = products(*rest, *all_weights), products(*two, *all_weights)
    out = [
        lax.dot_general(
            pick[a],
            jnp.concatenate([late[a], early[a]], axis=0).astype(BF),
            (((0,), (0,)), ((), ())),
            preferred_element_type=F32,
        ).astype(BF)
        for a in both
    ]
    out = jnp.stack(out)
    near_out = [shift_y(out[:, j * rows : (j + 1) * rows], j) for j in (1, 2, 3)]

    tok = jnp.stack([ordered[1][:, :feat], ordered[0][:, feat:]])
    tok2 = swap_core(tok)
    other_two = swap_core(jnp.stack([two[a][:, hid:] for a in both]))
    other_rest = swap_core(jnp.stack([rest[a][:, hid:] for a in both]))
    full = [
        jnp.concatenate([rest[a][:, :hid], two[a][:, :hid], other_rest[a], other_two[a]], axis=0)
        for a in both
    ]
    tokens = [jnp.concatenate([tok[k], tok2[k]], axis=0) for k in (0, 1)]

    def over_tokens(x, y):
        return lax.dot_general(x, y, (((0,), (0,)), ((), ())), preferred_element_type=F32).astype(BF)

    grads = (over_tokens(tokens[0], full[1]), over_tokens(full[0], tokens[1]))
    out, *grads = lax.optimization_barrier((out[:, :rows],) + grads)
    final = (out.astype(F32) + near_out[0] + near_out[1] + near_out[2]).astype(BF)
    return (final[0], final[1], *grads)


def solution(mesh):
    return jax.shard_map(
        shards,
        mesh=mesh,
        in_specs=(
            P("col", ("depth", "row")),
            P(("depth", "row"), "col"),
            P("col", ("depth", "row")),
            P("col", ("depth", "row")),
        ),
        out_specs=(
            P("col", ("depth", "row")),
            P("col", ("depth", "row")),
            P(("depth", "row"), "col"),
            P("col", ("depth", "row")),
        ),
        check_vma=False,
    )
```

```python
import functools

import jax
import jax.numpy as jnp
import numpy as np
from jax import lax
from jax.experimental import pallas as pl
from jax.experimental.pallas import tpu as pltpu
from jax.sharding import PartitionSpec as P

BF = jnp.bfloat16
F32 = jnp.float32


def gelu_pair(pre):
    coeff = 0.7978845608
    inner = coeff * (pre + 0.044715 * pre * pre * pre)
    tval = jnp.tanh(inner)
    value = 0.5 * pre * (1.0 + tval)
    slope = 0.5 * (1.0 + tval) + 0.5 * pre * (1.0 - tval * tval) * coeff * (
        1.0 + 3.0 * 0.044715 * pre * pre
    )
    return (value, slope)


def shift_y(x, k):
    return lax.ppermute(x, "col", [(i, (i + 2 * k) % 8) for i in range(8)])


def swap_core(x):
    return lax.ppermute(x, "col", [(i, i ^ 1) for i in range(8)])


def together(pair):
    return lax.optimization_barrier(tuple(pair))


def add(x, y):
    return (x.astype(F32) + y.astype(F32)).astype(BF)


def after(x, *others):
    return lax.optimization_barrier((x,) + others)[0]


PAIRS_X = ([1, 0, 3, 2], [3, 2, 1, 0])
PAIRS_Z = ([1, 0, 3, 2, 5, 4, 7, 6], [7, 2, 1, 4, 3, 6, 5, 0], [3, 6, 5, 0, 7, 2, 1, 4])
STEPS = (
    (("x", 0), ("x", 1), ("z", 0), ("z", 1), ("z", 2)),
    (("z", 0), ("z", 1), ("x", 0), ("x", 1), ("z", 2)),
)


def ring_of(i, array, n):
    return i if array == 0 else (n - i) % n


def partner_of(d, r, core, step, array):
    axis, k = STEPS[core][step]
    if axis == "x":
        return ring_of(PAIRS_X[k][ring_of(d, array, 4)], array, 4), r
    return d, ring_of(PAIRS_Z[k][ring_of(r, array, 8)], array, 8)


def order_of(d, r, core, array, step):
    if step == 5:
        return [d * 8 + r]
    return order_of(*partner_of(d, r, core, step, array), core, array, step + 1) + order_of(
        d, r, core, array, step + 1
    )


def orders():
    return np.array(
        [
            [
                [[order_of(d, r, core, array, 0) for array in (0, 1)] for r in range(8)]
                for d in range(4)
            ]
            for core in (0, 1)
        ],
        np.int32,
    )


def exchange(x, step, array):
    pairs = []
    for d in range(4):
        for r in range(8):
            for c in range(8):
                d2, r2 = partner_of(d, r, c % 2, step, array)
                pairs.append((d * 64 + r * 8 + c, d2 * 64 + r2 * 8 + c))
    return lax.ppermute(x, ("depth", "row", "col"), pairs)


MIB = 1024 * 1024


def small(limit=8):
    return pltpu.CompilerParams(vmem_limit_bytes=limit * MIB)


VMEM = pl.BlockSpec(memory_space=pltpu.VMEM)


def pack(inputs, grad_out):
    feat = inputs.shape[1]

    def body(x_ref, g_ref, out_ref):
        out_ref[:, :feat] = x_ref[...]
        out_ref[:, feat:] = g_ref[...]

    return pl.pallas_call(
        body,
        out_shape=jax.ShapeDtypeStruct((inputs.shape[0], 2 * feat), BF),
        compiler_params=small(4),
    )(inputs, grad_out)


def partials(tok, array, piece, w_here, w_there):
    rows = tok.shape[0] // 2
    hid = w_here.shape[1 - array]
    step = 768

    def body(tok_ref, here_ref, there_ref, out_ref):
        now = tok_ref[piece * rows : (piece + 1) * rows, :]
        for base, ref in ((0, here_ref), (hid, there_ref)):
            for i in range(0, hid, step):
                if array == 0:
                    value = jnp.dot(now, ref[:, i : i + step], preferred_element_type=F32)
                else:
                    value = lax.dot_general(
                        ref[i : i + step, :], now, (((1,), (1,)), ((), ())), preferred_element_type=F32
                    ).T
                out_ref[:, base + i : base + i + step] = value.astype(BF)

    return pl.pallas_call(
        body,
        in_specs=[VMEM] * 3,
        out_specs=VMEM,
        out_shape=jax.ShapeDtypeStruct((rows, 2 * hid), BF),
        cost_estimate=pl.CostEstimate(
            flops=4 * rows * w_here.size, bytes_accessed=4 * rows * hid, transcendentals=0
        ),
        compiler_params=small(16),
    )(tok, w_here, w_there)


def products(act, hidden_grad, w_in, w_in2, w_out, w_out2):
    rows, hid = act.shape[0], w_in.shape[1]
    feat = w_in.shape[0]

    def body(a_ref, h_ref, in_ref, in2_ref, out_w_ref, out2_ref, out_ref):
        out_ref[0] = jnp.dot(a_ref[:, :hid], out_w_ref[...], preferred_element_type=F32) + jnp.dot(
            a_ref[:, hid:], out2_ref[...], preferred_element_type=F32
        )
        turned = (((1,), (1,)), ((), ()))
        out_ref[1] = (
            lax.dot_general(in_ref[...], h_ref[:, :hid], turned, preferred_element_type=F32)
            + lax.dot_general(in2_ref[...], h_ref[:, hid:], turned, preferred_element_type=F32)
        ).T

    return pl.pallas_call(
        body,
        in_specs=[VMEM] * 6,
        out_specs=VMEM,
        out_shape=jax.ShapeDtypeStruct((2, rows, feat), F32),
        cost_estimate=pl.CostEstimate(
            flops=8 * rows * w_in.size, bytes_accessed=8 * rows * hid, transcendentals=0
        ),
        compiler_params=small(24),
    )(act, hidden_grad, w_in, w_in2, w_out, w_out2)


def shards(inputs, w_in, w_out, grad_out):
    x_at, z_at = lax.axis_index("depth"), lax.axis_index("row")
    core = lax.rem(lax.axis_index("col"), 2)
    rows, feat = inputs.shape
    hid = w_in.shape[1]
    both = (0, 1)

    own = pack(inputs, grad_out)
    w_in2, w_out2 = swap_core(w_in), swap_core(w_out)
    tokens = jnp.concatenate([own] + [shift_y(own, -j) for j in (1, 2, 3)], axis=0)
    order = jnp.asarray(orders())[core, x_at, z_at]
    size = 4 * rows // 32
    wanted = (order[:, :, None] * size + jnp.arange(size, dtype=jnp.int32)).reshape(2, 4 * rows)
    pick = (wanted[:, :, None] == jnp.arange(4 * rows, dtype=jnp.int32)).astype(BF)
    ordered = [jnp.dot(pick[a], tokens, preferred_element_type=F32).astype(BF) for a in both]
    tok = (ordered[0][:, :feat], ordered[1][:, feat:])
    weights = ((w_in, w_in2), (w_out, w_out2))
    send = [partials(tok[a], a, 0, *weights[a]) for a in both]
    keep = [partials(tok[a], a, 1, *weights[a]) for a in both]

    for step in range(5):
        got = [exchange(send[a], step, a) for a in both]
        if step < 1:
            got = together(got)
        left = keep[0].shape[0] // 2
        if step == 4:
            total = [keep[a].astype(F32) + got[a] for a in both]
        else:
            send = [add(keep[a][:left], got[a][:left]) for a in both]
            keep = [keep[a][left:].astype(F32) + got[a][left:] for a in both]

    value, slope = gelu_pair(total[0])
    held = [value.astype(BF), (total[1] * slope).astype(BF)]

    for step in (4, 3, 2, 1, 0):
        got = [exchange(held[a], step, a) for a in both]
        if step < 2:
            got = together(got)
        if step == 0:
            two, rest = held, got
        else:
            held = [jnp.concatenate([got[a], held[a]], axis=0) for a in both]

    all_weights = (w_in, w_in2, w_out, w_out2)
    late, early = products(*rest, *all_weights), products(*two, *all_weights)
    out = [
        lax.dot_general(
            pick[a],
            jnp.concatenate([late[a], early[a]], axis=0).astype(BF),
            (((0,), (0,)), ((), ())),
            preferred_element_type=F32,
        ).astype(BF)
        for a in both
    ]
    out = jnp.stack(out)
    near_out = [shift_y(out[:, j * rows : (j + 1) * rows], j) for j in (1, 2, 3)]

    tok = jnp.stack([ordered[1][:, :feat], ordered[0][:, feat:]])
    tok2 = swap_core(tok)
    other_two = swap_core(jnp.stack([two[a][:, hid:] for a in both]))
    other_rest = swap_core(jnp.stack([rest[a][:, hid:] for a in both]))
    full = [
        jnp.concatenate([rest[a][:, :hid], two[a][:, :hid], other_rest[a], other_two[a]], axis=0)
        for a in both
    ]
    tokens = [jnp.concatenate([tok[k], tok2[k]], axis=0) for k in (0, 1)]

    def over_tokens(x, y):
        return lax.dot_general(x, y, (((0,), (0,)), ((), ())), preferred_element_type=F32).astype(BF)

    grads = (over_tokens(tokens[0], full[1]), over_tokens(full[0], tokens[1]))
    out, *grads = lax.optimization_barrier((out[:, :rows],) + grads)
    final = (out.astype(F32) + near_out[0] + near_out[1] + near_out[2]).astype(BF)
    return (final[0], final[1], *grads)


def solution(mesh):
    return jax.shard_map(
        shards,
        mesh=mesh,
        in_specs=(
            P("col", ("depth", "row")),
            P(("depth", "row"), "col"),
            P("col", ("depth", "row")),
            P("col", ("depth", "row")),
        ),
        out_specs=(
            P("col", ("depth", "row")),
            P("col", ("depth", "row")),
            P(("depth", "row"), "col"),
            P("col", ("depth", "row")),
        ),
        check_vma=False,
    )
```
